32 devices in a mesh: groups: 2 (over x), vocab: 16 (over z, y, core).
Axes of the slice: x: 2, y: 2, z: 4, core: 2. Of those that a mesh axis runs over, the one named last changes fastest.
Arguments:
- policy_hidden: bfloat16 [128, 6144], P(('groups', 'vocab')), parts along dimension 0, may hold values from -250 to 250
- ref_hidden: bfloat16 [128, 6144], P(('groups', 'vocab')), parts along dimension 0, may hold values from -250 to 250
- policy_head: bfloat16 [6144, 16384], P(None, 'vocab'), may hold values from -0.25 to 0.25
- ref_head: bfloat16 [6144, 16384], P(None, 'vocab'), may hold values from -0.25 to 0.25
- lengths: int32 [2], P('groups'), parts along dimension 0, may hold values from 1 to 128
Outputs:
- kl_token: float32 [128], P(('groups', 'vocab')), parts along dimension 0
- hidden_grad: float32 [128, 6144], P(('groups', 'vocab')), parts along dimension 0
- head_grad: bfloat16 [12288, 16384], P('groups', 'vocab'), parts along dimension 0
The draws below stay inside these ranges and needn't reach their ends.
There are 2 independent parts, one for each index of `groups`. The reference program is written for one: setup_inputs(seed, part) draws one part's arguments, and reference() takes and returns one part's arrays. A program takes and returns all parts, laid end to end along the dimension named above; an argument that names none is the same for every part. Nothing has to cross between parts.
All inputs are finite; a program needn't handle non-finite values.
Results may differ from the reference program's by a relative error of at most 0.0054.
Values may be sent and summed in bfloat16 or wider, within the bound.
A program may use at most 128 MiB of HBM per device.

```python
import math
import jax
import jax.numpy as jnp

D = 6144
VOCAB = 16384
ROLL = 128
TOKENS = 64
ROWS = 1


def hidden_pair(key):
    first, second = jax.random.split(key, 2)
    base = jnp.clip(jax.random.normal(first, (TOKENS, D), jnp.float32), -6.0, 6.0)
    noise = jnp.clip(jax.random.normal(second, (TOKENS, D), jnp.float32), -6.0, 6.0)
    return (base, 0.9 * base + 0.45 * noise)


def head_pair(key):
    first, second = jax.random.split(key, 2)
    factor = 4.0 / math.sqrt(D)
    base = jnp.clip(jax.random.normal(first, (D, VOCAB), jnp.float32), -6.0, 6.0) * factor
    other = jnp.clip(jax.random.normal(second, (D, VOCAB), jnp.float32), -6.0, 6.0) * factor
    policy = jnp.clip(base, -0.25, 0.25)
    reference_head = jnp.clip(0.9 * base + 0.45 * other, -0.25, 0.25)
    return (policy, reference_head)


def draw_policy_hidden(key, part):
    policy, other = hidden_pair(key)
    return policy.astype(jnp.bfloat16)


def draw_ref_hidden(key, part):
    other, reference_rows = hidden_pair(key)
    return reference_rows.astype(jnp.bfloat16)


def draw_policy_head(key, part):
    policy, other = head_pair(key)
    return policy.astype(jnp.bfloat16)


def draw_ref_head(key, part):
    other, reference_head = head_pair(key)
    return reference_head.astype(jnp.bfloat16)


def setup_inputs(seed: int = 0, part: int = 0) -> dict:
    key_list = jax.random.split(jax.random.key(seed), 6)
    part_splits = jax.random.split(jax.random.fold_in(key_list[5], part), 6)
    policy_hidden = draw_policy_hidden(jax.random.fold_in(jax.random.fold_in(key_list[5], part), 71), part)
    ref_hidden = draw_ref_hidden(jax.random.fold_in(jax.random.fold_in(key_list[5], part), 71), part)
    policy_head = draw_policy_head(jax.random.fold_in(key_list[5], 71), part)
    ref_head = draw_ref_head(jax.random.fold_in(key_list[5], 71), part)
    lengths = jax.random.randint(part_splits[4], (ROWS,), 1, ROLL + 1).astype(jnp.int32)
    return dict(policy_hidden=policy_hidden, ref_hidden=ref_hidden, policy_head=policy_head, ref_head=ref_head, lengths=lengths)


def log_normalizer(logits):
    top = jnp.max(logits, axis=1, keepdims=True)
    return top + jnp.log(jnp.sum(jnp.exp(logits - top), axis=1, keepdims=True))


def reference(policy_hidden, ref_hidden, policy_head, ref_head, lengths):
    policy_logits = jnp.dot(policy_hidden, policy_head, preferred_element_type=jnp.float32)
    ref_logits = jnp.dot(ref_hidden, ref_head, preferred_element_type=jnp.float32)
    policy_logp = policy_logits - log_normalizer(policy_logits)
    ref_logp = ref_logits - log_normalizer(ref_logits)
    prob = jnp.exp(policy_logp)
    kl = jnp.sum(prob * (policy_logp - ref_logp), axis=1)
    positions = jnp.arange(TOKENS, dtype=jnp.int32)
    limits = lengths[positions // ROLL]
    token_mask = ((positions % ROLL) < limits).astype(jnp.float32)
    kl_token = token_mask * kl
    weights = token_mask / jnp.float32(ROLL * ROWS)
    grad_logits = (weights[:, None] * prob * ((policy_logp - ref_logp) - kl[:, None])).astype(jnp.bfloat16)
    hidden_grad = jnp.dot(grad_logits, policy_head.T, preferred_element_type=jnp.float32)
    head_grad = jnp.dot(policy_hidden.T, grad_logits, preferred_element_type=jnp.float32).astype(jnp.bfloat16)
    return kl_token, hidden_grad, head_grad
```

```python
import jax
import jax.numpy as jnp
from jax import lax
from jax.sharding import PartitionSpec as P

ROLL = 128


def body(policy_hidden, ref_hidden, policy_head, ref_head, lengths):
    tok_dev = policy_hidden.shape[0]
    tokens = tok_dev * lax.axis_size("vocab")
    stacked = jnp.stack((policy_hidden, ref_hidden))

    def logits_of(piece):
        return jnp.stack(
            (
                jnp.dot(piece[0], policy_head, preferred_element_type=jnp.float32),
                jnp.dot(piece[1], ref_head, preferred_element_type=jnp.float32),
            )
        )

    piece = lax.all_gather(stacked, "vocab", axis=1, tiled=True)
    both = logits_of(piece)
    policy_logits = both[0]
    ref_logits = both[1]
    own_top = jnp.max(policy_logits, axis=1)
    own_ref_top = jnp.max(ref_logits, axis=1)
    policy_exp = jnp.exp(policy_logits - own_top[:, None])
    stats = jnp.stack(
        (
            own_top,
            own_ref_top,
            jnp.sum(policy_exp, axis=1),
            jnp.sum(jnp.exp(ref_logits - own_ref_top[:, None]), axis=1),
            jnp.sum(policy_exp * (policy_logits - ref_logits), axis=1),
        )
    )
    stats = lax.all_gather(stats, "vocab", axis=0)
    policy_top = jnp.max(stats[:, 0], axis=0)
    ref_top = jnp.max(stats[:, 1], axis=0)
    policy_scale = jnp.exp(stats[:, 0] - policy_top)
    policy_sum = jnp.sum(stats[:, 2] * policy_scale, axis=0)
    ref_sum = jnp.sum(stats[:, 3] * jnp.exp(stats[:, 1] - ref_top), axis=0)
    numerator = jnp.sum(stats[:, 4] * policy_scale, axis=0)
    policy_lse = policy_top + jnp.log(policy_sum)
    ref_lse = ref_top + jnp.log(ref_sum)
    kl = numerator / policy_sum - policy_lse + ref_lse
    positions = jnp.arange(tokens, dtype=jnp.int32)
    row_count = lengths.shape[0]
    table = (positions // ROLL)[:, None] == jnp.arange(row_count, dtype=jnp.int32)[None, :]
    limits = jnp.sum(jnp.where(table, lengths[None, :], 0), axis=1)
    token_mask = (positions % ROLL < limits).astype(jnp.float32)
    weights = token_mask / jnp.float32(ROLL * row_count)
    own_first = lax.axis_index("vocab") * tok_dev
    kl_token = lax.dynamic_slice_in_dim(token_mask * kl, own_first, tok_dev)
    contract_rows = (((0,), (0,)), ((), ()))
    logits = both
    policy_logp = logits[0] - policy_lse[:, None]
    ref_logp = logits[1] - ref_lse[:, None]
    prob = jnp.exp(policy_logp)
    kl_rows = kl[:, None]
    weight_rows = weights[:, None]
    grad_piece = (weight_rows * prob * (policy_logp - ref_logp - kl_rows)).astype(jnp.bfloat16)
    head_total = lax.dot_general(
        piece[0], grad_piece, contract_rows, preferred_element_type=jnp.float32
    )
    accumulate_grad_table = grad_piece
    head_total, grad_table = (head_total, accumulate_grad_table)
    contract_vocab = (((1,), (1,)), ((), ()))
    grad_piece = grad_table
    hidden_grad = lax.psum_scatter(
        lax.dot_general(
            grad_piece, policy_head, contract_vocab, preferred_element_type=jnp.float32
        ),
        "vocab",
        scatter_dimension=0,
        tiled=True,
    )
    return (kl_token, hidden_grad, head_total.astype(jnp.bfloat16))


def solution(mesh):
    return jax.shard_map(
        body,
        mesh=mesh,
        in_specs=(
            P(("groups", "vocab"), None),
            P(("groups", "vocab"), None),
            P(None, "vocab"),
            P(None, "vocab"),
            P("groups"),
        ),
        out_specs=(P(("groups", "vocab")), P(("groups", "vocab"), None), P("groups", "vocab")),
        check_vma=False,
    )
```

```python
import functools

import jax
import jax.numpy as jnp
from jax import lax
from jax.experimental import pallas as pl
from jax.experimental.pallas import tpu as pltpu
from jax.sharding import PartitionSpec as P

ROLL = 128
TILE = 256
MESH = pl.DeviceIdType.MESH
F32 = jnp.float32
BF16 = jnp.bfloat16


def kernel(
    n,
    units,
    lengths,
    policy_head,
    ref_head,
    kl_out,
    hidden_out,
    grad_out,
    rows_out,
    gathered,
    ref_rows,
    policy_w,
    ref_w,
    policy_logits,
    ref_logits,
    stats,
    total,
    outgoing,
    sibling_in,
    ring_out,
    ring_in,
    head_sem,
    gather_send,
    gather_recv,
    stats_send,
    stats_recv,
    pair_send,
    pair_recv,
    ring_send,
    ring_recv,
):
    depth, columns = policy_w.shape
    half = depth // 2
    quarter = depth // 4
    eighth = depth // 8
    tokens = rows_out.shape[0]
    padded = stats.shape[2]
    chips = n // 2
    me = lax.axis_index("vocab")
    core = me % 2
    chip = me // 2
    snake = chips == 8

    def position_of(k):
        if not snake:
            return k
        z, y = k // 2, k % 2
        return (1 - y) * z + y * (chips - 1 - z)

    def chip_at(p):
        p = (p + chips) % chips
        if not snake:
            return p
        far = p // (chips // 2)
        return (1 - far) * 2 * p + far * (2 * (chips - 1 - p) + 1)

    pos = position_of(chip)
    right = chip_at(pos + 1) * 2 + core
    left = chip_at(pos - 1) * 2 + core
    sibling = chip * 2 + 1 - core

    longer, shorter = chips // 2, chips - 1 - chips // 2
    limits = ((longer, shorter), (shorter, longer))

    head_copies = []
    for j in range(2):
        span = pl.ds(j * half, half)
        for which, (hbm, vmem) in enumerate(((policy_head, policy_w), (ref_head, ref_w))):
            copy = pltpu.make_async_copy(hbm.at[span], vmem.at[span], head_sem.at[j, which])
            copy.start()
            head_copies.append(copy)

    barrier = pltpu.get_barrier_semaphore()

    def greet(i, carry):
        pl.semaphore_signal(
            barrier, inc=1, device_id={"vocab": (me + i) % n}, device_id_type=MESH
        )
        return carry

    lax.fori_loop(1, n, greet, 0)
    pl.semaphore_wait(barrier, n - 1)

    sent = []

    def remote(src, dst, send, recv, device):
        return pltpu.make_async_remote_copy(
            src_ref=src,
            dst_ref=dst,
            send_sem=send,
            recv_sem=recv,
            device_id={"vocab": device},
            device_id_type=MESH,
        )

    def send(src, dst, send_sem, recv_sem, device):
        copy = remote(src, dst, send_sem, recv_sem, device)
        copy.start()
        sent.append(copy)

    def pass_on(j, src, owner, lane, step, device):
        send(
            src,
            gathered.at[j, owner],
            gather_send.at[j, lane, step],
            gather_recv.at[j, owner],
            device,
        )

    def arrived(j, owner):
        slot = gathered.at[j, owner]
        remote(slot, slot, gather_send.at[j, 0, 0], gather_recv.at[j, owner], sibling).wait_recv()

    for j in range(2):
        pass_on(j, units.at[j], me, 0, 0, right)
        pass_on(j, units.at[j], me, 1, 0, left)
        pass_on(j, units.at[j], me, 2, 0, sibling)
    for j in range(2):
        gathered[j, me] = units[j]
    for step in range(1, longer + 1):
        for j in range(2):
            for way in range(2):
                limit = limits[way][j]
                if step > limit:
                    continue
                owner = chip_at(pos - step if way == 0 else pos + step) * 2 + core
                arrived(j, owner)
                if step < limit:
                    pass_on(j, gathered.at[j, owner], owner, way, step, (right, left)[way])
                lane = 2 + way
                pass_on(j, gathered.at[j, owner], owner, lane, step, sibling)

    low = lax.broadcasted_iota(jnp.int32, (8, quarter), 0) < 4
    for j in range(2):
        for k in range(chips):
            arrived(j, k * 2 + 1 - core)
        for group in range(n // 4):
            block = gathered[j, 4 * group : 4 * group + 4].astype(F32)
            for q in range(2):
                part = block[:, 8 * q : 8 * q + 8]
                policy, ref = [], []
                for i in range(2):
                    even, odd = part[2 * i], part[2 * i + 1]
                    policy.append(jnp.where(low, even, pltpu.roll(odd, 4, 0)))
                    ref.append(jnp.where(low, pltpu.roll(even, 4, 0), odd))
                span = pl.ds(j * half + q * quarter, quarter)
                rows = pl.ds(16 * group, 16)
                rows_out[rows, span] = jnp.concatenate(policy, axis=0).astype(BF16)
                ref_rows[rows, span] = jnp.concatenate(ref, axis=0).astype(BF16)
        head_copies[2 * j].wait()
        head_copies[2 * j + 1].wait()
        span = pl.ds(j * half, half)

        @pl.loop(0, columns // TILE)
        def _(i, j=j, span=span):
            cols = pl.ds(pl.multiple_of(i * TILE, TILE), TILE)
            for x, w, out in (
                (rows_out, policy_w, policy_logits),
                (ref_rows, ref_w, ref_logits),
            ):
                product = jnp.dot(x[:, span], w[span, cols], preferred_element_type=F32)
                out[:, cols] = product if j == 0 else out[:, cols] + product

    p, r = policy_logits[...], ref_logits[...]
    p_top = jnp.max(p, axis=1, keepdims=True)
    r_top = jnp.max(r, axis=1, keepdims=True)
    p_exp = jnp.exp(p - p_top)
    p_sum = jnp.sum(p_exp, axis=1, keepdims=True)
    r_sum = jnp.sum(jnp.exp(r - r_top), axis=1, keepdims=True)
    numerator = jnp.sum(p_exp * (p - r), axis=1, keepdims=True)
    lane = lax.broadcasted_iota(jnp.int32, (tokens, 128), 1)
    table = jnp.zeros((tokens, 128), F32)
    for i, column in ((0, p_top), (1, r_top), (2, p_top), (4, p_sum), (5, r_sum), (6, numerator)):
        table = jnp.where(lane == i, column, table)
    if padded > tokens:
        table = jnp.concatenate([table, jnp.ones((padded - tokens, 128), F32)], axis=0)
    stats[me] = table.T[:8]

    def stats_copy(i):
        target = (me + i) % n
        return remote(
            stats.at[me], stats.at[me], stats_send.at[i], stats_recv.at[me], target
        )

    def spread(i, carry):
        stats_copy(i).start()
        return carry

    def collect(i, carry):
        source = (me + n - i) % n
        slot = stats.at[source]
        remote(slot, slot, stats_send.at[i], stats_recv.at[source], source).wait_recv()
        stats_copy(i).wait_send()
        return carry

    lax.fori_loop(1, n, spread, 0)
    lax.fori_loop(1, n, collect, 0)

    top = stats[0]
    for d in range(1, n):
        top = jnp.maximum(top, stats[d])
    sums = jnp.zeros_like(top)
    for d in range(n):
        one = stats[d]
        sums = sums + pltpu.roll(jnp.exp(one - top), 4, 0) * one
    p_lse = top[0:1] + jnp.log(sums[4:5])
    r_lse = top[1:2] + jnp.log(sums[5:6])
    kl = sums[6:7] / sums[4:5] - p_lse + r_lse
    token = lax.broadcasted_iota(jnp.int32, (1, padded), 1)
    row = token // ROLL
    row_count = lengths.shape[0]
    limit = jnp.zeros((1, padded), jnp.int32)
    for i in range(row_count):
        limit = jnp.where(row == i, lengths[i], limit)
    mask = (token - row * ROLL < limit).astype(F32)
    weight = mask / jnp.float32(ROLL * row_count)
    kl_out[...] = mask * kl
    line = lax.broadcasted_iota(jnp.int32, (128, padded), 0)
    table = jnp.where(line == 0, p_lse, jnp.where(line == 1, r_lse, jnp.where(line == 2, kl, weight)))
    table = table.T[:tokens]
    p_lse, r_lse, kl, weight = (table[:, i : i + 1] for i in range(4))

    p_logp = policy_logits[...] - p_lse
    r_logp = ref_logits[...] - r_lse
    grad_out[...] = (weight * jnp.exp(p_logp) * ((p_logp - r_logp) - kl)).astype(BF16)

    low = lax.broadcasted_iota(jnp.int32, (chips, 8, TILE), 1) < 4
    for j in range(2):

        @pl.loop(0, eighth // TILE)
        def _(i, j=j):
            cols = pl.ds(pl.multiple_of(i * TILE, TILE), TILE)
            outs = []
            for a in range(4):
                start = pl.multiple_of(j * half + a * eighth + i * TILE, TILE)
                outs.append(
                    lax.dot_general(
                        grad_out[...],
                        policy_w[pl.ds(start, TILE), :],
                        (((1,), (1,)), ((), ())),
                        preferred_element_type=F32,
                    ).reshape(chips, 8, TILE)
                )
            for c in range(2):
                halves = []
                for a in (0, 2):
                    first, second = outs[a], outs[a + 1]
                    if c == 0:
                        second = pltpu.roll(second, 4, 1)
                    else:
                        first = pltpu.roll(first, 4, 1)
                    halves.append(jnp.where(low, first, second))
                both = jnp.concatenate(halves, axis=1)
                total[j, c, :, :, cols] = both
                outgoing[j, c, :, :, cols] = both.astype(BF16)

        send(
            outgoing.at[j, 1 - core],
            sibling_in.at[j],
            pair_send.at[j],
            pair_recv.at[j],
            sibling,
        )

    def own(j, k):
        return total[j, core, k] + sibling_in[j, k].astype(F32)

    def ring_wait(j, way, step):
        slot = ring_in.at[j, way, step]
        remote(
            slot, slot, ring_send.at[j, way, step], ring_recv.at[j, way, step], sibling
        ).wait_recv()

    for step in range(longer):
        for j in range(2):
            if step == 0:
                remote(
                    sibling_in.at[j], sibling_in.at[j], pair_send.at[j], pair_recv.at[j], sibling
                ).wait_recv()
            for way in range(2):
                limit = limits[way][j]
                if step >= limit:
                    continue
                hops = limit - step
                value = own(j, chip_at(pos + hops if way == 0 else pos - hops))
                if step > 0:
                    ring_wait(j, way, step - 1)
                    value = value + ring_in[j, way, step - 1].astype(F32)
                ring_out[j, way, step] = value.astype(BF16)
                send(
                    ring_out.at[j, way, step],
                    ring_in.at[j, way, step],
                    ring_send.at[j, way, step],
                    ring_recv.at[j, way, step],
                    (right, left)[way],
                )
    for j in range(2):
        value = own(j, chip)
        for way in range(2):
            last = limits[way][j] - 1
            ring_wait(j, way, last)
            value = value + ring_in[j, way, last].astype(F32)
        hidden_out[j] = value
    for copy in sent:
        copy.wait_send()


def body(policy_hidden, ref_hidden, policy_head, ref_head, lengths):
    n = lax.axis_size("vocab")
    tok_dev, depth = policy_hidden.shape
    columns = policy_head.shape[1]
    tokens = tok_dev * n
    chips = n // 2
    padded = -(-tokens // 128) * 128
    steps = chips // 2 + 1
    quarter, eighth = depth // 4, depth // 8
    units = jnp.concatenate((policy_hidden, ref_hidden), axis=0)
    units = units.reshape(8, 2, 2, quarter).transpose(1, 2, 0, 3).reshape(2, 16, quarter)
    vmem = pl.BlockSpec(memory_space=pltpu.VMEM)
    hbm = pl.BlockSpec(memory_space=pl.ANY)
    dma = pltpu.SemaphoreType.DMA
    kl, hidden, grad, rows = pl.pallas_call(
        functools.partial(kernel, n),
        out_shape=(
            jax.ShapeDtypeStruct((1, padded), F32),
            jax.ShapeDtypeStruct((2, 16, eighth), F32),
            jax.ShapeDtypeStruct((tokens, columns), BF16),
            jax.ShapeDtypeStruct((tokens, depth), BF16),
        ),
        in_specs=[vmem, pl.BlockSpec(memory_space=pltpu.SMEM), hbm, hbm],
        out_specs=(vmem,) * 4,
        scratch_shapes=[
            pltpu.VMEM((2, n, 16, quarter), BF16),
            pltpu.VMEM((tokens, depth), BF16),
            pltpu.VMEM((depth, columns), BF16),
            pltpu.VMEM((depth, columns), BF16),
            pltpu.VMEM((tokens, columns), F32),
            pltpu.VMEM((tokens, columns), F32),
            pltpu.VMEM((n, 8, padded), F32),
            pltpu.VMEM((2, 2, chips, 16, eighth), F32),
            pltpu.VMEM((2, 2, chips, 16, eighth), BF16),
            pltpu.VMEM((2, chips, 16, eighth), BF16),
            pltpu.VMEM((2, 2, steps, 16, eighth), BF16),
            pltpu.VMEM((2, 2, steps, 16, eighth), BF16),
            dma((2, 2)),
            dma((2, 4, steps)),
            dma((2, n)),
            dma((n,)),
            dma((n,)),
            dma((2,)),
            dma((2,)),
            dma((2, 2, steps)),
            dma((2, 2, steps)),
        ],
        compiler_params=pltpu.CompilerParams(
            collective_id=0, has_side_effects=True, vmem_limit_bytes=56 * 2**20
        ),
    )(units, lengths, policy_head, ref_head)
    own_first = lax.axis_index("vocab") * tok_dev
    kl_token = lax.dynamic_slice_in_dim(kl[0], own_first, tok_dev)
    hidden_grad = (
        hidden.reshape(2, 4, tok_dev, eighth).transpose(2, 0, 1, 3).reshape(tok_dev, depth)
    )
    head_grad = lax.dot_general(
        rows, grad, (((0,), (0,)), ((), ())), preferred_element_type=F32
    ).astype(BF16)
    return kl_token, hidden_grad, head_grad


def solution(mesh):
    return jax.shard_map(
        body,
        mesh=mesh,
        in_specs=(
            P(("groups", "vocab"), None),
            P(("groups", "vocab"), None),
            P(None, "vocab"),
            P(None, "vocab"),
            P("groups"),
        ),
        out_specs=(P(("groups", "vocab")), P(("groups", "vocab"), None), P("groups", "vocab")),
        check_vma=False,
    )
```

```python
import functools

import jax
import jax.numpy as jnp
from jax import lax
from jax.experimental import pallas as pl
from jax.experimental.pallas import tpu as pltpu
from jax.sharding import PartitionSpec as P

ROLL = 128
TILE = 256
MESH = pl.DeviceIdType.MESH
F32 = jnp.float32
BF16 = jnp.bfloat16


def kernel(
    n,
    policy_hidden,
    ref_hidden,
    lengths,
    policy_head,
    ref_head,
    kl_out,
    hidden_out,
    grad_out,
    rows_out,
    gathered,
    ref_rows,
    policy_w,
    ref_w,
    policy_logits,
    ref_logits,
    stats,
    total,
    outgoing,
    sibling_in,
    ring_out,
    ring_in,
    head_sem,
    gather_send,
    gather_recv,
    stats_send,
    stats_recv,
    pair_send,
    pair_recv,
    ring_send,
    ring_recv,
):
    depth, columns = policy_w.shape
    half = depth // 2
    quarter = depth // 4
    eighth = depth // 8
    tokens = rows_out.shape[0]
    padded = stats.shape[2]
    chips = n // 2
    me = lax.axis_index("vocab")
    core = me % 2
    chip = me // 2
    snake = chips == 8

    def position_of(k):
        if not snake:
            return k
        z, y = k // 2, k % 2
        return (1 - y) * z + y * (chips - 1 - z)

    def chip_at(p):
        p = (p + chips) % chips
        if not snake:
            return p
        far = p // (chips // 2)
        return (1 - far) * 2 * p + far * (2 * (chips - 1 - p) + 1)

    pos = position_of(chip)
    right = chip_at(pos + 1) * 2 + core
    left = chip_at(pos - 1) * 2 + core
    sibling = chip * 2 + 1 - core

    longer, shorter = chips // 2, chips - 1 - chips // 2
    limits = ((longer, shorter), (shorter, longer))

    head_copies = []
    for j in range(2):
        span = pl.ds(j * half, half)
        for which, (hbm, vmem) in enumerate(((policy_head, policy_w), (ref_head, ref_w))):
            copy = pltpu.make_async_copy(hbm.at[span], vmem.at[span], head_sem.at[j, which])
            copy.start()
            head_copies.append(copy)

    barrier = pltpu.get_barrier_semaphore()

    def greet(i, carry):
        pl.semaphore_signal(
            barrier, inc=1, device_id={"vocab": (me + i) % n}, device_id_type=MESH
        )
        return carry

    lax.fori_loop(1, n, greet, 0)
    for j in range(2):
        for q in range(2):
            span = pl.ds(j * half + q * quarter, quarter)
            both = jnp.concatenate(
                (policy_hidden[:, span].astype(F32), ref_hidden[:, span].astype(F32)), axis=0
            )
            gathered[j, me, 8 * q : 8 * q + 8] = both.astype(BF16)
    pl.semaphore_wait(barrier, n - 1)

    sent = []

    def remote(src, dst, send, recv, device):
        return pltpu.make_async_remote_copy(
            src_ref=src,
            dst_ref=dst,
            send_sem=send,
            recv_sem=recv,
            device_id={"vocab": device},
            device_id_type=MESH,
        )

    def send(src, dst, send_sem, recv_sem, device):
        copy = remote(src, dst, send_sem, recv_sem, device)
        copy.start()
        sent.append(copy)

    def pass_on(j, src, owner, lane, step, device):
        send(
            src,
            gathered.at[j, owner],
            gather_send.at[j, lane, step],
            gather_recv.at[j, owner],
            device,
        )

    def arrived(j, owner):
        slot = gathered.at[j, owner]
        remote(slot, slot, gather_send.at[j, 0, 0], gather_recv.at[j, owner], sibling).wait_recv()

    for j in range(2):
        pass_on(j, gathered.at[j, me], me, 0, 0, right)
        pass_on(j, gathered.at[j, me], me, 1, 0, left)
        pass_on(j, gathered.at[j, me], me, 2, 0, sibling)
    for step in range(1, longer + 1):
        for j in range(2):
            for way in range(2):
                limit = limits[way][j]
                if step > limit:
                    continue
                owner = chip_at(pos - step if way == 0 else pos + step) * 2 + core
                arrived(j, owner)
                if step < limit:
                    pass_on(j, gathered.at[j, owner], owner, way, step, (right, left)[way])
                lane = 2 + way
                pass_on(j, gathered.at[j, owner], owner, lane, step, sibling)

    low = lax.broadcasted_iota(jnp.int32, (8, quarter), 0) < 4
    for j in range(2):
        for k in range(chips):
            arrived(j, k * 2 + 1 - core)
        for group in range(n // 4):
            block = gathered[j, 4 * group : 4 * group + 4].astype(F32)
            for q in range(2):
                part = block[:, 8 * q : 8 * q + 8]
                policy, ref = [], []
                for i in range(2):
                    even, odd = part[2 * i], part[2 * i + 1]
                    policy.append(jnp.where(low, even, pltpu.roll(odd, 4, 0)))
                    ref.append(jnp.where(low, pltpu.roll(even, 4, 0), odd))
                span = pl.ds(j * half + q * quarter, quarter)
                rows = pl.ds(16 * group, 16)
                rows_out[rows, span] = jnp.concatenate(policy, axis=0).astype(BF16)
                ref_rows[rows, span] = jnp.concatenate(ref, axis=0).astype(BF16)
        head_copies[2 * j].wait()
        head_copies[2 * j + 1].wait()
        span = pl.ds(j * half, half)

        @pl.loop(0, columns // TILE)
        def _(i, j=j, span=span):
            cols = pl.ds(pl.multiple_of(i * TILE, TILE), TILE)
            for x, w, out in (
                (rows_out, policy_w, policy_logits),
                (ref_rows, ref_w, ref_logits),
            ):
                product = jnp.dot(x[:, span], w[span, cols], preferred_element_type=F32)
                out[:, cols] = product if j == 0 else out[:, cols] + product

    p, r = policy_logits[...], ref_logits[...]
    p_top = jnp.max(p, axis=1, keepdims=True)
    r_top = jnp.max(r, axis=1, keepdims=True)
    p_exp = jnp.exp(p - p_top)
    p_sum = jnp.sum(p_exp, axis=1, keepdims=True)
    r_sum = jnp.sum(jnp.exp(r - r_top), axis=1, keepdims=True)
    numerator = jnp.sum(p_exp * (p - r), axis=1, keepdims=True)
    lane = lax.broadcasted_iota(jnp.int32, (tokens, 128), 1)
    table = jnp.zeros((tokens, 128), F32)
    for i, column in ((0, p_top), (1, r_top), (2, p_top), (4, p_sum), (5, r_sum), (6, numerator)):
        table = jnp.where(lane == i, column, table)
    if padded > tokens:
        table = jnp.concatenate([table, jnp.ones((padded - tokens, 128), F32)], axis=0)
    stats[me] = table.T[:8]

    def stats_copy(i):
        target = (me + i) % n
        return remote(
            stats.at[me], stats.at[me], stats_send.at[i], stats_recv.at[me], target
        )

    def spread(i, carry):
        stats_copy(i).start()
        return carry

    def collect(i, carry):
        source = (me + n - i) % n
        slot = stats.at[source]
        remote(slot, slot, stats_send.at[i], stats_recv.at[source], source).wait_recv()
        stats_copy(i).wait_send()
        return carry

    lax.fori_loop(1, n, spread, 0)
    lax.fori_loop(1, n, collect, 0)

    top = stats[0]
    for d in range(1, n):
        top = jnp.maximum(top, stats[d])
    sums = jnp.zeros_like(top)
    for d in range(n):
        one = stats[d]
        sums = sums + pltpu.roll(jnp.exp(one - top), 4, 0) * one
    p_lse = top[0:1] + jnp.log(sums[4:5])
    r_lse = top[1:2] + jnp.log(sums[5:6])
    kl = sums[6:7] / sums[4:5] - p_lse + r_lse
    token = lax.broadcasted_iota(jnp.int32, (1, padded), 1)
    row = token // ROLL
    row_count = lengths.shape[0]
    limit = jnp.zeros((1, padded), jnp.int32)
    for i in range(row_count):
        limit = jnp.where(row == i, lengths[i], limit)
    mask = (token - row * ROLL < limit).astype(F32)
    weight = mask / jnp.float32(ROLL * row_count)
    kl_out[...] = mask * kl
    line = lax.broadcasted_iota(jnp.int32, (128, padded), 0)
    table = jnp.where(line == 0, p_lse, jnp.where(line == 1, r_lse, jnp.where(line == 2, kl, weight)))
    table = table.T[:tokens]
    p_lse, r_lse, kl, weight = (table[:, i : i + 1] for i in range(4))

    p_logp = policy_logits[...] - p_lse
    r_logp = ref_logits[...] - r_lse
    grad_out[...] = (weight * jnp.exp(p_logp) * ((p_logp - r_logp) - kl)).astype(BF16)

    low = lax.broadcasted_iota(jnp.int32, (chips, 8, TILE), 1) < 4
    for j in range(2):

        @pl.loop(0, eighth // TILE)
        def _(i, j=j):
            cols = pl.ds(pl.multiple_of(i * TILE, TILE), TILE)
            outs = []
            for a in range(4):
                start = pl.multiple_of(j * half + a * eighth + i * TILE, TILE)
                outs.append(
                    lax.dot_general(
                        grad_out[...],
                        policy_w[pl.ds(start, TILE), :],
                        (((1,), (1,)), ((), ())),
                        preferred_element_type=F32,
                    ).reshape(chips, 8, TILE)
                )
            for c in range(2):
                halves = []
                for a in (0, 2):
                    first, second = outs[a], outs[a + 1]
                    if c == 0:
                        second = pltpu.roll(second, 4, 1)
                    else:
                        first = pltpu.roll(first, 4, 1)
                    halves.append(jnp.where(low, first, second))
                both = jnp.concatenate(halves, axis=1)
                total[j, c, :, :, cols] = both
                outgoing[j, c, :, :, cols] = both.astype(BF16)

        send(
            outgoing.at[j, 1 - core],
            sibling_in.at[j],
            pair_send.at[j],
            pair_recv.at[j],
            sibling,
        )

    def own(j, k):
        return total[j, core, k] + sibling_in[j, k].astype(F32)

    def ring_wait(j, way, step):
        slot = ring_in.at[j, way, step]
        remote(
            slot, slot, ring_send.at[j, way, step], ring_recv.at[j, way, step], sibling
        ).wait_recv()

    for step in range(longer):
        for j in range(2):
            if step == 0:
                remote(
                    sibling_in.at[j], sibling_in.at[j], pair_send.at[j], pair_recv.at[j], sibling
                ).wait_recv()
            for way in range(2):
                limit = limits[way][j]
                if step >= limit:
                    continue
                hops = limit - step
                value = own(j, chip_at(pos + hops if way == 0 else pos - hops))
                if step > 0:
                    ring_wait(j, way, step - 1)
                    value = value + ring_in[j, way, step - 1].astype(F32)
                ring_out[j, way, step] = value.astype(BF16)
                send(
                    ring_out.at[j, way, step],
                    ring_in.at[j, way, step],
                    ring_send.at[j, way, step],
                    ring_recv.at[j, way, step],
                    (right, left)[way],
                )
    for j in range(2):
        value = own(j, chip)
        for way in range(2):
            last = limits[way][j] - 1
            ring_wait(j, way, last)
            value = value + ring_in[j, way, last].astype(F32)
        hidden_out[j] = value
    for copy in sent:
        copy.wait_send()


def finish(rows, grad, hidden, kl, head_out, hidden_out, kl_out):
    head_out[...] = lax.dot_general(
        rows[...], grad[...], (((0,), (0,)), ((), ())), preferred_element_type=F32
    ).astype(BF16)

    @pl.when(pl.program_id(0) == 0)
    def _():
        tok_dev = kl_out.shape[0]
        width = hidden.shape[2]
        for j in range(2):
            for a in range(4):
                start = (4 * j + a) * width
                hidden_out[:, start : start + width] = hidden[
                    j, a * tok_dev : (a + 1) * tok_dev
                ]
        first = lax.axis_index("vocab") * tok_dev
        padded = kl.shape[1]
        whole = jnp.broadcast_to(kl[...], (8, padded))
        turned = pltpu.roll(whole, lax.rem(padded - first, padded), 1)
        kl_out[...] = turned[0, :tok_dev]


def body(policy_hidden, ref_hidden, policy_head, ref_head, lengths):
    n = lax.axis_size("vocab")
    tok_dev, depth = policy_hidden.shape
    columns = policy_head.shape[1]
    tokens = tok_dev * n
    chips = n // 2
    padded = -(-tokens // 128) * 128
    steps = chips // 2 + 1
    quarter, eighth = depth // 4, depth // 8
    vmem = pl.BlockSpec(memory_space=pltpu.VMEM)
    hbm = pl.BlockSpec(memory_space=pl.ANY)
    dma = pltpu.SemaphoreType.DMA
    kl, hidden, grad, rows = pl.pallas_call(
        functools.partial(kernel, n),
        out_shape=(
            jax.ShapeDtypeStruct((1, padded), F32),
            jax.ShapeDtypeStruct((2, 16, eighth), F32),
            jax.ShapeDtypeStruct((tokens, columns), BF16),
            jax.ShapeDtypeStruct((tokens, depth), BF16),
        ),
        in_specs=[vmem, vmem, pl.BlockSpec(memory_space=pltpu.SMEM), hbm, hbm],
        out_specs=(vmem,) * 4,
        scratch_shapes=[
            pltpu.VMEM((2, n, 16, quarter), BF16),
            pltpu.VMEM((tokens, depth), BF16),
            pltpu.VMEM((depth, columns), BF16),
            pltpu.VMEM((depth, columns), BF16),
            pltpu.VMEM((tokens, columns), F32),
            pltpu.VMEM((tokens, columns), F32),
            pltpu.VMEM((n, 8, padded), F32),
            pltpu.VMEM((2, 2, chips, 16, eighth), F32),
            pltpu.VMEM((2, 2, chips, 16, eighth), BF16),
            pltpu.VMEM((2, chips, 16, eighth), BF16),
            pltpu.VMEM((2, 2, steps, 16, eighth), BF16),
            pltpu.VMEM((2, 2, steps, 16, eighth), BF16),
            dma((2, 2)),
            dma((2, 4, steps)),
            dma((2, n)),
            dma((n,)),
            dma((n,)),
            dma((2,)),
            dma((2,)),
            dma((2, 2, steps)),
            dma((2, 2, steps)),
        ],
        compiler_params=pltpu.CompilerParams(
            collective_id=0, has_side_effects=True, vmem_limit_bytes=56 * 2**20
        ),
    )(policy_hidden, ref_hidden, lengths, policy_head, ref_head)
    block = 512
    head_grad, hidden_grad, kl_token = pl.pallas_call(
        finish,
        grid=(depth // block,),
        in_specs=[
            pl.BlockSpec((tokens, block), lambda i: (0, i)),
            pl.BlockSpec((tokens, columns), lambda i: (0, 0)),
            pl.BlockSpec(hidden.shape, lambda i: (0, 0, 0)),
            pl.BlockSpec((1, padded), lambda i: (0, 0)),
        ],
        out_specs=(
            pl.BlockSpec((block, columns), lambda i: (i, 0)),
            pl.BlockSpec((tok_dev, depth), lambda i: (0, 0)),
            pl.BlockSpec((tok_dev,), lambda i: (0,)),
        ),
        out_shape=(
            jax.ShapeDtypeStruct((depth, columns), BF16),
            jax.ShapeDtypeStruct((tok_dev, depth), F32),
            jax.ShapeDtypeStruct((tok_dev,), F32),
        ),
        compiler_params=pltpu.CompilerParams(vmem_limit_bytes=32 * 2**20),
    )(rows, grad, hidden, kl)
    return kl_token, hidden_grad, head_grad


def solution(mesh):
    return jax.shard_map(
        body,
        mesh=mesh,
        in_specs=(
            P(("groups", "vocab"), None),
            P(("groups", "vocab"), None),
            P(None, "vocab"),
            P(None, "vocab"),
            P("groups"),
        ),
        out_specs=(P(("groups", "vocab")), P(("groups", "vocab"), None), P("groups", "vocab")),
        check_vma=False,
    )
```

```python
import functools

import jax
import jax.numpy as jnp
from jax import lax
from jax.experimental import pallas as pl
from jax.experimental.pallas import tpu as pltpu
from jax.sharding import PartitionSpec as P

ROLL = 128
TILE = 256
MESH = pl.DeviceIdType.MESH
F32 = jnp.float32
BF16 = jnp.bfloat16


def kernel(
    n,
    policy_hidden,
    ref_hidden,
    lengths,
    policy_head,
    ref_head,
    kl_out,
    hidden_out,
    grad_out,
    rows_out,
    gathered,
    ref_rows,
    policy_w,
    ref_w,
    policy_logits,
    ref_logits,
    stats,
    total,
    outgoing,
    sibling_in,
    ring_out,
    ring_in,
    head_sem,
    gather_send,
    gather_recv,
    stats_send,
    stats_recv,
    pair_send,
    pair_recv,
    ring_send,
    ring_recv,
):
    depth, columns = policy_w.shape
    half = depth // 2
    quarter = depth // 4
    eighth = depth // 8
    tokens = rows_out.shape[0]
    padded = stats.shape[2]
    chips = n // 2
    me = lax.axis_index("vocab")
    core = me % 2
    chip = me // 2
    snake = chips == 8

    def position_of(k):
        if not snake:
            return k
        z, y = k // 2, k % 2
        return (1 - y) * z + y * (chips - 1 - z)

    def chip_at(p):
        p = (p + chips) % chips
        if not snake:
            return p
        far = p // (chips // 2)
        return (1 - far) * 2 * p + far * (2 * (chips - 1 - p) + 1)

    pos = position_of(chip)
    right = chip_at(pos + 1) * 2 + core
    left = chip_at(pos - 1) * 2 + core
    sibling = chip * 2 + 1 - core

    longer, shorter = chips // 2, chips - 1 - chips // 2
    limits = ((longer, shorter), (shorter, longer))

    head_copies = []
    for j in range(2):
        span = pl.ds(j * half, half)
        for which, (hbm, vmem) in enumerate(((policy_head, policy_w), (ref_head, ref_w))):
            copy = pltpu.make_async_copy(hbm.at[span], vmem.at[span], head_sem.at[j, which])
            copy.start()
            head_copies.append(copy)

    barrier = pltpu.get_barrier_semaphore()

    def greet(i, carry):
        pl.semaphore_signal(
            barrier, inc=1, device_id={"vocab": (me + i) % n}, device_id_type=MESH
        )
        return carry

    lax.fori_loop(1, n, greet, 0)
    for j in range(2):
        for q in range(2):
            span = pl.ds(j * half + q * quarter, quarter)
            both = jnp.concatenate(
                (policy_hidden[:, span].astype(F32), ref_hidden[:, span].astype(F32)), axis=0
            )
            gathered[j, me, 8 * q : 8 * q + 8] = both.astype(BF16)
    pl.semaphore_wait(barrier, n - 1)

    sent = []

    def remote(src, dst, send, recv, device):
        return pltpu.make_async_remote_copy(
            src_ref=src,
            dst_ref=dst,
            send_sem=send,
            recv_sem=recv,
            device_id={"vocab": device},
            device_id_type=MESH,
        )

    def send(src, dst, send_sem, recv_sem, device):
        copy = remote(src, dst, send_sem, recv_sem, device)
        copy.start()
        sent.append(copy)

    def pass_on(j, src, owner, lane, step, device):
        send(
            src,
            gathered.at[j, owner],
            gather_send.at[j, lane, step],
            gather_recv.at[j, owner],
            device,
        )

    def arrived(j, owner):
        slot = gathered.at[j, owner]
        remote(slot, slot, gather_send.at[j, 0, 0], gather_recv.at[j, owner], sibling).wait_recv()

    for j in range(2):
        pass_on(j, gathered.at[j, me], me, 0, 0, right)
        pass_on(j, gathered.at[j, me], me, 1, 0, left)
        pass_on(j, gathered.at[j, me], me, 2, 0, sibling)
    for step in range(1, longer + 1):
        for j in range(2):
            for way in range(2):
                limit = limits[way][j]
                if step > limit:
                    continue
                owner = chip_at(pos - step if way == 0 else pos + step) * 2 + core
                arrived(j, owner)
                if step < limit:
                    pass_on(j, gathered.at[j, owner], owner, way, step, (right, left)[way])
                lane = 2 + way
                pass_on(j, gathered.at[j, owner], owner, lane, step, sibling)

    low = lax.broadcasted_iota(jnp.int32, (8, quarter), 0) < 4
    for j in range(2):
        for k in range(chips):
            arrived(j, k * 2 + 1 - core)
        for group in range(n // 4):
            block = gathered[j, 4 * group : 4 * group + 4].astype(F32)
            for q in range(2):
                part = block[:, 8 * q : 8 * q + 8]
                policy, ref = [], []
                for i in range(2):
                    even, odd = part[2 * i], part[2 * i + 1]
                    policy.append(jnp.where(low, even, pltpu.roll(odd, 4, 0)))
                    ref.append(jnp.where(low, pltpu.roll(even, 4, 0), odd))
                span = pl.ds(j * half + q * quarter, quarter)
                rows = pl.ds(16 * group, 16)
                rows_out[rows, span] = jnp.concatenate(policy, axis=0).astype(BF16)
                ref_rows[rows, span] = jnp.concatenate(ref, axis=0).astype(BF16)
        head_copies[2 * j].wait()
        head_copies[2 * j + 1].wait()
        span = pl.ds(j * half, half)

        @pl.loop(0, columns // TILE)
        def _(i, j=j, span=span):
            cols = pl.ds(pl.multiple_of(i * TILE, TILE), TILE)
            for x, w, out in (
                (rows_out, policy_w, policy_logits),
                (ref_rows, ref_w, ref_logits),
            ):
                product = jnp.dot(x[:, span], w[span, cols], preferred_element_type=F32)
                out[:, cols] = product if j == 0 else out[:, cols] + product

    p, r = policy_logits[...], ref_logits[...]
    p_top = jnp.max(p, axis=1, keepdims=True)
    r_top = jnp.max(r, axis=1, keepdims=True)
    p_exp = jnp.exp(p - p_top)
    p_sum = jnp.sum(p_exp, axis=1, keepdims=True)
    r_sum = jnp.sum(jnp.exp(r - r_top), axis=1, keepdims=True)
    numerator = jnp.sum(p_exp * (p - r), axis=1, keepdims=True)
    lane = lax.broadcasted_iota(jnp.int32, (tokens, 128), 1)
    table = jnp.zeros((tokens, 128), F32)
    for i, column in ((0, p_top), (1, r_top), (2, p_top), (4, p_sum), (5, r_sum), (6, numerator)):
        table = jnp.where(lane == i, column, table)
    if padded > tokens:
        table = jnp.concatenate([table, jnp.ones((padded - tokens, 128), F32)], axis=0)
    stats[me] = table.T[:8]

    def stats_copy(i):
        target = (me + i) % n
        return remote(
            stats.at[me], stats.at[me], stats_send.at[i], stats_recv.at[me], target
        )

    def spread(i, carry):
        stats_copy(i).start()
        return carry

    def collect(i, carry):
        source = (me + n - i) % n
        slot = stats.at[source]
        remote(slot, slot, stats_send.at[i], stats_recv.at[source], source).wait_recv()
        stats_copy(i).wait_send()
        return carry

    lax.fori_loop(1, n, spread, 0)
    lax.fori_loop(1, n, collect, 0)

    top = stats[0]
    for d in range(1, n):
        top = jnp.maximum(top, stats[d])
    sums = jnp.zeros_like(top)
    for d in range(n):
        one = stats[d]
        sums = sums + pltpu.roll(jnp.exp(one - top), 4, 0) * one
    p_lse = top[0:1] + jnp.log(sums[4:5])
    r_lse = top[1:2] + jnp.log(sums[5:6])
    kl = sums[6:7] / sums[4:5] - p_lse + r_lse
    token = lax.broadcasted_iota(jnp.int32, (1, padded), 1)
    row = token // ROLL
    row_count = lengths.shape[0]
    limit = jnp.zeros((1, padded), jnp.int32)
    for i in range(row_count):
        limit = jnp.where(row == i, lengths[i], limit)
    mask = (token - row * ROLL < limit).astype(F32)
    weight = mask / jnp.float32(ROLL * row_count)
    kl_out[...] = mask * kl
    line = lax.broadcasted_iota(jnp.int32, (128, padded), 0)
    table = jnp.where(line == 0, p_lse, jnp.where(line == 1, r_lse, jnp.where(line == 2, kl, weight)))
    table = table.T[:tokens]
    p_lse, r_lse, kl, weight = (table[:, i : i + 1] for i in range(4))

    p_logp = policy_logits[...] - p_lse
    r_logp = ref_logits[...] - r_lse
    grad_out[...] = (weight * jnp.exp(p_logp) * ((p_logp - r_logp) - kl)).astype(BF16)

    low = lax.broadcasted_iota(jnp.int32, (chips, 8, TILE), 1) < 4
    def share(j, first, last):
        @pl.loop(first, last)
        def _(i):
            cols = pl.ds(pl.multiple_of(i * TILE, TILE), TILE)
            outs = []
            for a in range(4):
                start = pl.multiple_of(j * half + a * eighth + i * TILE, TILE)
                outs.append(
                    lax.dot_general(
                        grad_out[...],
                        policy_w[pl.ds(start, TILE), :],
                        (((1,), (1,)), ((), ())),
                        preferred_element_type=F32,
                    ).reshape(chips, 8, TILE)
                )
            for c in range(2):
                halves = []
                for a in (0, 2):
                    first, second = outs[a], outs[a + 1]
                    if c == 0:
                        second = pltpu.roll(second, 4, 1)
                    else:
                        first = pltpu.roll(first, 4, 1)
                    halves.append(jnp.where(low, first, second))
                both = jnp.concatenate(halves, axis=1)
                total[j, c, :, :, cols] = both
                outgoing[j, c, :, :, cols] = both.astype(BF16)

    def pair_start(j):
        send(
            outgoing.at[j, 1 - core],
            sibling_in.at[j],
            pair_send.at[j],
            pair_recv.at[j],
            sibling,
        )

    def own(j, k):
        return total[j, core, k] + sibling_in[j, k].astype(F32)

    def ring_wait(j, way, step):
        slot = ring_in.at[j, way, step]
        remote(
            slot, slot, ring_send.at[j, way, step], ring_recv.at[j, way, step], sibling
        ).wait_recv()

    def ring_step(j, step):
        if step == 0:
            remote(
                sibling_in.at[j], sibling_in.at[j], pair_send.at[j], pair_recv.at[j], sibling
            ).wait_recv()
        for way in range(2):
            limit = limits[way][j]
            if step >= limit:
                continue
            hops = limit - step
            value = own(j, chip_at(pos + hops if way == 0 else pos - hops))
            if step > 0:
                ring_wait(j, way, step - 1)
                value = value + ring_in[j, way, step - 1].astype(F32)
            ring_out[j, way, step] = value.astype(BF16)
            send(
                ring_out.at[j, way, step],
                ring_in.at[j, way, step],
                ring_send.at[j, way, step],
                ring_recv.at[j, way, step],
                (right, left)[way],
            )
    tiles = eighth // TILE
    share(0, 0, tiles)
    pair_start(0)
    for i in range(tiles):
        share(1, i, i + 1)
        if i == tiles - 1:
            pair_start(1)
        if i < longer:
            ring_step(0, i)
    for step in range(longer):
        ring_step(1, step)
        if step + tiles < longer:
            ring_step(0, step + tiles)
    for j in range(2):
        value = own(j, chip)
        for way in range(2):
            last = limits[way][j] - 1
            ring_wait(j, way, last)
            value = value + ring_in[j, way, last].astype(F32)
        hidden_out[j] = value
    for copy in sent:
        copy.wait_send()


def finish(rows, grad, hidden, kl, head_out, hidden_out, kl_out):
    head_out[...] = lax.dot_general(
        rows[...], grad[...], (((0,), (0,)), ((), ())), preferred_element_type=F32
    ).astype(BF16)

    @pl.when(pl.program_id(0) == 0)
    def _():
        tok_dev = kl_out.shape[0]
        width = hidden.shape[2]
        for j in range(2):
            for a in range(4):
                start = (4 * j + a) * width
                hidden_out[:, start : start + width] = hidden[
                    j, a * tok_dev : (a + 1) * tok_dev
                ]
        first = lax.axis_index("vocab") * tok_dev
        padded = kl.shape[1]
        whole = jnp.broadcast_to(kl[...], (8, padded))
        turned = pltpu.roll(whole, lax.rem(padded - first, padded), 1)
        kl_out[...] = turned[0, :tok_dev]


def body(policy_hidden, ref_hidden, policy_head, ref_head, lengths):
    n = lax.axis_size("vocab")
    tok_dev, depth = policy_hidden.shape
    columns = policy_head.shape[1]
    tokens = tok_dev * n
    chips = n // 2
    padded = -(-tokens // 128) * 128
    steps = chips // 2 + 1
    quarter, eighth = depth // 4, depth // 8
    vmem = pl.BlockSpec(memory_space=pltpu.VMEM)
    hbm = pl.BlockSpec(memory_space=pl.ANY)
    dma = pltpu.SemaphoreType.DMA
    kl, hidden, grad, rows = pl.pallas_call(
        functools.partial(kernel, n),
        out_shape=(
            jax.ShapeDtypeStruct((1, padded), F32),
            jax.ShapeDtypeStruct((2, 16, eighth), F32),
            jax.ShapeDtypeStruct((tokens, columns), BF16),
            jax.ShapeDtypeStruct((tokens, depth), BF16),
        ),
        in_specs=[vmem, vmem, pl.BlockSpec(memory_space=pltpu.SMEM), hbm, hbm],
        out_specs=(vmem,) * 4,
        scratch_shapes=[
            pltpu.VMEM((2, n, 16, quarter), BF16),
            pltpu.VMEM((tokens, depth), BF16),
            pltpu.VMEM((depth, columns), BF16),
            pltpu.VMEM((depth, columns), BF16),
            pltpu.VMEM((tokens, columns), F32),
            pltpu.VMEM((tokens, columns), F32),
            pltpu.VMEM((n, 8, padded), F32),
            pltpu.VMEM((2, 2, chips, 16, eighth), F32),
            pltpu.VMEM((2, 2, chips, 16, eighth), BF16),
            pltpu.VMEM((2, chips, 16, eighth), BF16),
            pltpu.VMEM((2, 2, steps, 16, eighth), BF16),
            pltpu.VMEM((2, 2, steps, 16, eighth), BF16),
            dma((2, 2)),
            dma((2, 4, steps)),
            dma((2, n)),
            dma((n,)),
            dma((n,)),
            dma((2,)),
            dma((2,)),
            dma((2, 2, steps)),
            dma((2, 2, steps)),
        ],
        compiler_params=pltpu.CompilerParams(
            collective_id=0, has_side_effects=True, vmem_limit_bytes=56 * 2**20
        ),
    )(policy_hidden, ref_hidden, lengths, policy_head, ref_head)
    block = 512
    head_grad, hidden_grad, kl_token = pl.pallas_call(
        finish,
        grid=(depth // block,),
        in_specs=[
            pl.BlockSpec((tokens, block), lambda i: (0, i)),
            pl.BlockSpec((tokens, columns), lambda i: (0, 0)),
            pl.BlockSpec(hidden.shape, lambda i: (0, 0, 0)),
            pl.BlockSpec((1, padded), lambda i: (0, 0)),
        ],
        out_specs=(
            pl.BlockSpec((block, columns), lambda i: (i, 0)),
            pl.BlockSpec((tok_dev, depth), lambda i: (0, 0)),
            pl.BlockSpec((tok_dev,), lambda i: (0,)),
        ),
        out_shape=(
            jax.ShapeDtypeStruct((depth, columns), BF16),
            jax.ShapeDtypeStruct((tok_dev, depth), F32),
            jax.ShapeDtypeStruct((tok_dev,), F32),
        ),
        compiler_params=pltpu.CompilerParams(vmem_limit_bytes=32 * 2**20),
    )(rows, grad, hidden, kl)
    return kl_token, hidden_grad, head_grad


def solution(mesh):
    return jax.shard_map(
        body,
        mesh=mesh,
        in_specs=(
            P(("groups", "vocab"), None),
            P(("groups", "vocab"), None),
            P(None, "vocab"),
            P(None, "vocab"),
            P("groups"),
        ),
        out_specs=(P(("groups", "vocab")), P(("groups", "vocab"), None), P("groups", "vocab")),
        check_vma=False,
    )
```
